32 devices in a mesh: region: 8 (over y, x, core), tile: 4 (over z).
Axes of the slice: x: 2, y: 2, z: 4, core: 2. Of those that a mesh axis runs over, the one named last changes fastest.
Arguments:
- state: float32 [80, 4, 16384], P(None, 'tile', 'region'), may hold values from -6 to 6
- obs_rows: float32 [8, 80, 4, 128], P('region', None, 'tile'), may hold values from -6 to 6
- obs_value: float32 [8, 4, 128], P('region', 'tile'), may hold values from -6 to 6
- obs_noise: float32 [8, 4, 128], P('region', 'tile'), may hold values from 0.3 to 3
- obs_cell: int32 [8, 4, 128], P('region', 'tile'), may hold values from 0 to 16383
- obs_class: int32 [8, 4, 128], P('region', 'tile'), may hold values from 0 to 2
- obs_count: int32 [8, 4], P('region', 'tile'), may hold values from 1 to 128, 256 in all within a row
Outputs:
- posterior: float32 [80, 4, 16384], P(None, 'tile', 'region')
The draws below stay inside these ranges and needn't reach their ends.
Inputs may be any that keep to these rules, and one draw needn't show every extreme that they name: `obs_count`: in every batch some tile has exactly 128 live slots.
All inputs are finite; a program needn't handle non-finite values. No bound on the sum of `obs_count` on one device may be relied on, other than what follows from the above.
Results may differ from the reference program's by a relative error of at most 0.0003.
Values sent between devices are 32-bit elements; how exact they have to be, the bound alone decides.
A program may use at most 64 MiB of HBM per device.

```python
import math
import jax
import jax.numpy as jnp
import numpy as np
from jax import lax

M = 80
K_DEV = 128
TILES = 4
BATCHES = 8
TILE_CELLS = 16384


def place_ends(array, rng, smallest, largest):
    longest = array.shape.index(max(array.shape))
    spots = []
    for shift in (0, 1):
        where = [jax.random.randint(jax.random.fold_in(rng, axis), (), 0, length) for axis, length in enumerate(array.shape)]
        where[longest] = (where[longest] + shift) % array.shape[longest]
        spots.append(tuple(where))
    return array.at[spots[0]].set(smallest).at[spots[1]].set(largest)


def shard_levels(stream_key, dims, pieces, least, top_value):
    loudness = 1.0
    for axis_at, blocks in pieces:
        steps = jax.random.uniform(jax.random.fold_in(jax.random.fold_in(stream_key, 6), axis_at), (blocks,), jnp.float32, least / len(pieces), top_value / len(pieces))
        loudness = loudness * jnp.repeat(jnp.exp(steps), dims[axis_at] // blocks).reshape((-1,) + (1,) * (len(dims) - 1 - axis_at))
    return loudness


def profile(number_of, total, reach, skew):
    weights = [(1 << 20) // math.isqrt(rank ** skew) + 1 for rank in range(2, number_of + 1)]
    rest, holding = total - reach - (number_of - 1), [1] * (number_of - 1)
    while rest > 0:
        candidates = [i for i in range(number_of - 1) if holding[i] < reach]
        pool, left = sum([weights[i] for i in candidates]), rest
        for i in candidates:
            extra = min(reach - holding[i], max(1, left * weights[i] // pool), rest)
            holding[i] = holding[i] + extra
            rest = rest - extra
    return np.array([reach] + holding)


def uneven(own_key, number_of, total, most, slope):
    if number_of == 2:
        one = jax.random.randint(own_key, (), max(1, total - most), min(most, total - 1) + 1)
        return jnp.stack([one, total - one])
    sizes = jnp.asarray(profile(number_of, total, most, slope), jnp.int32)
    couples = (number_of - 1) // 2
    source_of, sink = sizes[1:1 + 2 * couples:2], sizes[2:2 + 2 * couples:2]
    room = jnp.minimum(source_of - 1, most - sink)
    shifted = jax.random.randint(jax.random.fold_in(own_key, 1), (couples,), 0, 1 << 20) % (room + 1)
    sizes = sizes.at[1:1 + 2 * couples:2].set(source_of - shifted).at[2:2 + 2 * couples:2].set(sink + shifted)
    return sizes[jax.random.permutation(jax.random.fold_in(own_key, 2), number_of)]


def normal_values(rng, shape, scale, reach, split=(), kind=jnp.bfloat16):
    factor_of = shard_levels(rng, shape, split, -0.22, 0.18) if split else 1.0
    values = jax.random.normal(rng, shape, jnp.float32) * scale * factor_of
    return jnp.minimum(jnp.maximum(values, -reach), reach).astype(kind)


def setup_inputs(seed: int = 0) -> dict:
    key_list = jax.random.split(jax.random.key(seed), 8)
    return {
        "state": normal_values(key_list[0], (M, TILES, TILE_CELLS), 1.0, 6.0, ((1, 4), (2, 8)), jnp.float32),
        "obs_rows": normal_values(key_list[1], (BATCHES, M, TILES, K_DEV), 1.0, 6.0, ((0, 8), (2, 4)), jnp.float32),
        "obs_value": normal_values(key_list[2], (BATCHES, TILES, K_DEV), 1.5, 6.0, ((0, 8), (1, 4)), jnp.float32),
        "obs_noise": jnp.clip(jnp.exp(math.log(3.0) - 2.3025851 * jax.random.uniform(key_list[3], (BATCHES, TILES, K_DEV), jnp.float32) ** shard_levels(key_list[3], (BATCHES, TILES, K_DEV), ((0, 8), (1, 4)), -0.2, 0.2)), 0.3, 3.0),
        "obs_cell": place_ends(jax.random.randint(key_list[4], (BATCHES, TILES, K_DEV), 0, TILE_CELLS), jax.random.fold_in(key_list[4], 1), 0, TILE_CELLS - 1).astype(jnp.int32),
        "obs_class": place_ends(jax.random.randint(key_list[5], (BATCHES, TILES, K_DEV), 0, 3), jax.random.fold_in(key_list[5], 1), 0, 2).astype(jnp.int32),
        "obs_count": jax.vmap(lambda own: uneven(own, TILES, TILES * K_DEV // 2, K_DEV, 2))(jax.random.split(key_list[6], BATCHES)).reshape((BATCHES, TILES)).astype(jnp.int32),
    }


PRECISE = lax.Precision.HIGHEST
EPSILON = 1e-06
DIMS_CROSS = (((0,), (0,)), ((), ()))
DIMS_APPLY = (((1,), (1,)), ((), ()))

def taper(distance, inv_width):
    nearness = jnp.maximum(1.0 - distance * inv_width, 0.0)
    return nearness * nearness

def batch_terms(rows_now, obs_val, noise_var, live_mask):
    members = rows_now.shape[0]
    ens_mean = lax.optimization_barrier(jnp.mean(rows_now, axis=0))
    anomaly = rows_now - ens_mean[None]
    prior_var = lax.optimization_barrier(jnp.sum(anomaly * anomaly, axis=0)) / (members - 1) + EPSILON
    post_var = 1.0 / (1.0 / prior_var + 1.0 / noise_var)
    post_mean = post_var * (ens_mean / prior_var + obs_val / noise_var)
    shift_term = jnp.where(live_mask, post_mean - ens_mean, 0.0)
    factor = jnp.where(live_mask, jnp.sqrt(post_var / prior_var) - 1.0, 0.0)
    obs_scale = 1.0 / ((members - 1) * prior_var)
    return (anomaly, shift_term, factor, obs_scale)

def regress(target, target_pos, anomaly, increment, obs_scale, source_pos, inv_width):
    centered = target - lax.optimization_barrier(jnp.mean(target, axis=0))[None]
    covariance = lax.dot_general(centered, anomaly, DIMS_CROSS, precision=PRECISE, preferred_element_type=jnp.float32)
    weights = taper(jnp.abs(target_pos[:, None] - source_pos[None, :]), inv_width[None, :])
    gain = weights * (covariance * obs_scale[None, :])
    return target + lax.dot_general(increment, gain, DIMS_APPLY, precision=PRECISE, preferred_element_type=jnp.float32)

def pad_tiles(values):
    spec = [(0, 0)] * (values.ndim - 2) + [(1, 1), (0, 0)]
    return jnp.pad(values, spec)

def reference(state, obs_rows, obs_value, obs_noise, obs_cell, obs_class, obs_count):
    members, tiles, tile_width = state.shape
    nbatch = obs_rows.shape[0]
    slot_count = obs_rows.shape[3]
    tile_start = jnp.arange(tiles, dtype=jnp.int32) * tile_width
    cell_pos = (tile_start[:, None] + jnp.arange(tile_width, dtype=jnp.int32)[None, :]).astype(jnp.float32)
    obs_pos = (tile_start[None, :, None] + obs_cell).astype(jnp.float32)
    inv_width = 4.0 / (tile_width * (obs_class + 2).astype(jnp.float32))
    live_all = jnp.arange(slot_count, dtype=jnp.int32)[None, None, :] < obs_count[:, :, None]
    current = obs_rows
    for batch_step in range(nbatch):
        anomaly, shift_term, factor, obs_scale = batch_terms(current[batch_step], obs_value[batch_step], obs_noise[batch_step], live_all[batch_step])
        increment = shift_term[None] + factor[None] * anomaly
        anomaly_pad = pad_tiles(anomaly)
        increment_pad = pad_tiles(increment)
        scale_pad = pad_tiles(obs_scale)
        pos_pad = pad_tiles(obs_pos[batch_step])
        inv_pad = pad_tiles(inv_width[batch_step])
        state_now = state
        rows_now = current

        def one_tile(tile_index):

            def pick_tiles(values):
                return lax.dynamic_slice_in_dim(values, tile_index, 3, values.ndim - 2)
            src_anomaly = pick_tiles(anomaly_pad).reshape(members, 3 * slot_count)
            src_increment = pick_tiles(increment_pad).reshape(members, 3 * slot_count)
            src_scale = pick_tiles(scale_pad).reshape(3 * slot_count)
            src_pos = pick_tiles(pos_pad).reshape(3 * slot_count)
            src_inv = pick_tiles(inv_pad).reshape(3 * slot_count)
            tile_cells = lax.dynamic_index_in_dim(state_now, tile_index, 1, False)
            tile_rows = lax.dynamic_index_in_dim(rows_now, tile_index, 2, False)
            tile_rows = jnp.transpose(tile_rows, (1, 0, 2)).reshape(members, nbatch * slot_count)
            target = jnp.concatenate([tile_cells, tile_rows], axis=1)
            row_pos = lax.dynamic_index_in_dim(obs_pos, tile_index, 1, False).reshape(nbatch * slot_count)
            target_pos = jnp.concatenate([lax.dynamic_index_in_dim(cell_pos, tile_index, 0, False), row_pos])
            return regress(target, target_pos, src_anomaly, src_increment, src_scale, src_pos, src_inv)
        result = lax.map(one_tile, jnp.arange(tiles, dtype=jnp.int32))
        state = jnp.transpose(result[:, :, :tile_width], (1, 0, 2))
        new_rows = result[:, :, tile_width:].reshape(tiles, members, nbatch, slot_count)
        new_rows = jnp.transpose(new_rows, (2, 1, 0, 3))
        later_mask = (jnp.arange(nbatch, dtype=jnp.int32) > batch_step)[:, None, None, None]
        current = jnp.where(later_mask, new_rows, current)
    return state
```

```python
import functools

import jax
import jax.numpy as jnp
from jax import lax
from jax.experimental import pallas as pl
from jax.experimental.pallas import tpu as pltpu
from jax.sharding import PartitionSpec as P

EPSILON = 1e-06
LANES = 256
GROUP = 2
F32 = jnp.float32
BF16 = jnp.bfloat16


def split(x):
    high = x.astype(BF16)
    return high, (x - high.astype(F32)).astype(BF16)


def kernel(nbatch, tiles, members, width, scal_ref, obs_ref, state_ref, out_ref,
           z_ref, pos_ref, info_ref, lhs_ref, inc_ref, pk_ref, wk_ref):
    slots = obs_ref.shape[2]
    rows = obs_ref.shape[1]
    cells = state_ref.shape[1]
    first = nbatch * width
    total = first + cells
    depth = lhs_ref.shape[1]
    pad = depth - 3 * members
    lane = lax.broadcasted_iota(jnp.int32, (1, width), 1)

    def compact(b, carry):
        acc = jnp.zeros((rows, width), F32)
        start = jnp.int32(0)
        for t in range(tiles):
            count = scal_ref[b * tiles + t]
            x = obs_ref[b * tiles + t]
            x = jnp.concatenate([x, jnp.zeros((rows, width - slots), F32)], axis=1)
            x = pltpu.roll(x, start, 1)
            here = (lane >= start) & (lane < start + count)
            acc = jnp.where(here, x, acc)
            start = start + count
        cols = pl.ds(pl.multiple_of(b * width, width), width)
        z_ref[:, cols] = acc[:members]
        info_ref[b] = acc[members:]
        pos_ref[:, cols] = jnp.broadcast_to(acc[members + 2 : members + 3], (8, width))
        return carry

    lax.fori_loop(0, nbatch, compact, 0)
    z_ref[:, first:] = state_ref[...]
    cell = scal_ref[nbatch * tiles] + lax.broadcasted_iota(jnp.int32, (8, cells), 1)
    pos_ref[:, first:] = cell.astype(F32)

    def step(b, carry):
        cols = pl.ds(pl.multiple_of(b * width, width), width)
        now = z_ref[:, cols]
        info = info_ref[b]
        value, noise = info[0:1], info[1:2]
        mean = jnp.sum(now, axis=0, keepdims=True) / members
        anomaly = now - mean
        prior = jnp.sum(anomaly * anomaly, axis=0, keepdims=True) / (members - 1) + EPSILON
        post = 1.0 / (1.0 / prior + 1.0 / noise)
        shift = post * (mean / prior + value / noise) - mean
        factor = jnp.sqrt(post / prior) - 1.0
        increment = shift + factor * anomaly
        inc_high, inc_low = split(increment)
        inc_ref[...] = jnp.concatenate([inc_high, inc_low], axis=0)
        scaled = anomaly * (1.0 / ((members - 1) * prior))
        high = scaled.astype(BF16).astype(F32)
        stacked = jnp.concatenate(
            [high, high, scaled - high, jnp.zeros((pad, width), F32)], axis=0
        )
        lhs_ref[...] = jnp.transpose(stacked).astype(BF16)
        turned = jnp.transpose(jnp.concatenate([info] * 16, axis=0))
        pk_ref[...] = jnp.broadcast_to(turned[:, 2:3], (width, LANES))
        wk_ref[...] = jnp.broadcast_to(turned[:, 3:4], (width, LANES))

        def group(g, inner):
            base = g * (GROUP * LANES)
            spans = [
                pl.ds(pl.multiple_of(base + i * LANES, LANES), LANES) for i in range(GROUP)
            ]
            values = [z_ref[:, span] for span in spans]
            places = [pos_ref[0:1, span] for span in spans]
            lhs = lhs_ref[...]
            inc = inc_ref[...]
            results = []
            for z, place in zip(values, places):
                centered = z - jnp.sum(z, axis=0, keepdims=True) / members
                z_high, z_low = split(centered)
                rhs = jnp.concatenate(
                    [z_high, z_low, z_high, jnp.zeros((pad, LANES), BF16)], axis=0
                )
                cov = jnp.dot(lhs, rhs, preferred_element_type=F32)
                near = jnp.maximum(1.0 - jnp.abs(place - pk_ref[...]) * wk_ref[...], 0.0)
                gain_high, gain_low = split(near * near * cov)
                both = jnp.dot(inc, gain_high, preferred_element_type=F32)
                low = jnp.dot(inc[:members], gain_low, preferred_element_type=F32)
                results.append(z + (both[:members] + (both[members:] + low)))
            for span, result in zip(spans, results):
                z_ref[:, span] = result
            return inner

        lax.fori_loop(((b + 1) * width) // (GROUP * LANES), total // (GROUP * LANES), group, 0)
        return carry

    lax.fori_loop(0, nbatch, step, 0)
    out_ref[...] = z_ref[:, first:]


def on_device(state, obs_rows, obs_value, obs_noise, obs_cell, obs_class, obs_count):
    members = state.shape[0]
    cells = state.shape[2]
    slots = obs_rows.shape[3]
    nbatch = lax.axis_size("region")
    tiles = lax.axis_size("tile")
    region_index = lax.axis_index("region")
    tile_index = lax.axis_index("tile")
    tile_width = cells * nbatch
    width = tiles * slots // 2
    depth = -(-3 * members // 128) * 128
    own_pos = (tile_index * tile_width + obs_cell[0]).astype(F32)
    own_inv = 4.0 / (tile_width * (obs_class[0] + 2).astype(F32))
    count_row = jnp.broadcast_to(obs_count.astype(F32), (1, slots))
    packed = jnp.concatenate(
        [obs_rows[0, :, 0, :], obs_value[0], obs_noise[0], own_pos, own_inv, count_row,
         jnp.zeros((3, slots), F32)], axis=0
    )
    rows = packed.shape[0]
    gathered = lax.all_gather(packed, ("region", "tile"), axis=0)
    counts = gathered[:, members + 4, 0].astype(jnp.int32)
    base = (tile_index * tile_width + region_index * cells).astype(jnp.int32)
    scalars = jnp.concatenate([counts, base[None]])
    total = nbatch * width + cells
    vmem = pl.BlockSpec(memory_space=pltpu.VMEM)
    out = pl.pallas_call(
        functools.partial(kernel, nbatch, tiles, members, width),
        out_shape=jax.ShapeDtypeStruct((members, cells), F32),
        in_specs=[pl.BlockSpec(memory_space=pltpu.SMEM), vmem, vmem],
        out_specs=vmem,
        scratch_shapes=[
            pltpu.VMEM((members, total), F32),
            pltpu.VMEM((8, total), F32),
            pltpu.VMEM((nbatch, rows - members, width), F32),
            pltpu.VMEM((width, depth), BF16),
            pltpu.VMEM((2 * members, width), BF16),
            pltpu.VMEM((width, LANES), F32),
            pltpu.VMEM((width, LANES), F32),
        ],
        compiler_params=pltpu.CompilerParams(vmem_limit_bytes=40 * 1024 * 1024),
    )(scalars, gathered, state[:, 0, :])
    return out[:, None, :]


def solution(mesh):
    placed = (
        P(None, "tile", "region"),
        P("region", None, "tile", None),
        P("region", "tile", None),
        P("region", "tile", None),
        P("region", "tile", None),
        P("region", "tile", None),
        P("region", "tile"),
    )
    return jax.shard_map(
        on_device, mesh=mesh, in_specs=placed, out_specs=P(None, "tile", "region"), check_vma=False
    )
```

```python
import functools

import jax
import jax.numpy as jnp
from jax import lax
from jax.experimental import pallas as pl
from jax.experimental.pallas import tpu as pltpu
from jax.sharding import PartitionSpec as P

EPSILON = 1e-06
LANES = 256
GROUP = 2
F32 = jnp.float32
BF16 = jnp.bfloat16


def split(x):
    high = x.astype(BF16)
    return high, (x - high.astype(F32)).astype(BF16)


def gather_kernel(nbatch, tiles, members, width, tile_width, count_ref, rows_ref, value_ref,
                  noise_ref, cell_ref, class_ref, out_ref, own_ref, slab_ref, live_ref,
                  tile_send, tile_recv, region_send, region_recv, local_sem):
    region = lax.axis_index("region")
    tile = lax.axis_index("tile")
    slots = rows_ref.shape[1]
    barrier = pltpu.get_barrier_semaphore()
    for i in range(1, tiles):
        pl.semaphore_signal(barrier, inc=1, device_id=(region, lax.rem(tile + i, tiles)),
                            device_id_type=pl.DeviceIdType.MESH)
    for i in range(1, nbatch):
        pl.semaphore_signal(barrier, inc=1, device_id=(lax.rem(region + i, nbatch), tile),
                            device_id_type=pl.DeviceIdType.MESH)

    spot = (tile * tile_width + cell_ref[...]).astype(F32)
    inv = 4.0 / (tile_width * (class_ref[...] + 2).astype(F32))
    count = jnp.full((1, slots), count_ref[0, 0], jnp.int32).astype(F32)
    own_ref[0:members] = rows_ref[...]
    own_ref[members:] = jnp.concatenate(
        [value_ref[...], noise_ref[...], spot, inv, count, jnp.zeros((own_ref.shape[0] - members - 5, slots), F32)], axis=0
    )
    pl.semaphore_wait(barrier, tiles + nbatch - 2)

    copies = []
    for i in range(1, tiles):
        copy = pltpu.make_async_remote_copy(
            src_ref=own_ref, dst_ref=slab_ref.at[tile],
            send_sem=tile_send.at[i], recv_sem=tile_recv.at[i],
            device_id=(region, lax.rem(tile + i, tiles)),
            device_id_type=pl.DeviceIdType.MESH)
        copy.start()
        copies.append(copy)
    slab_ref[tile] = own_ref[...]
    for copy in copies:
        copy.wait()

    lane = lax.broadcasted_iota(jnp.int32, (1, slots), 1).astype(F32)
    row = lax.broadcasted_iota(jnp.int32, (width, slots), 0).astype(F32)
    start = jnp.zeros((1, slots), F32)
    picks, parts = [], []
    for t in range(tiles):
        block = slab_ref[t]
        count = block[members + 4 : members + 5]
        place = jnp.where(lane < count, start + lane, -1.0)
        picks.append(jnp.where(row == place, 1.0, 0.0).astype(BF16))
        start = start + count
        high = block.astype(BF16)
        rest = block - high.astype(F32)
        middle, low = split(rest)
        parts.append(jnp.concatenate([high, middle, low], axis=0))
    moved = lax.dot_general(
        jnp.concatenate(parts, axis=1), jnp.concatenate(picks, axis=1),
        (((1,), (1,)), ((), ())), preferred_element_type=F32)
    count_rows = own_ref.shape[0]
    live_ref[...] = moved[:count_rows] + (
        moved[count_rows : 2 * count_rows] + moved[2 * count_rows : 3 * count_rows])

    copies = [pltpu.make_async_copy(live_ref, out_ref.at[region], local_sem)]
    for i in range(1, nbatch):
        copies.append(pltpu.make_async_remote_copy(
            src_ref=live_ref, dst_ref=out_ref.at[region],
            send_sem=region_send.at[i], recv_sem=region_recv.at[i],
            device_id=(lax.rem(region + i, nbatch), tile),
            device_id_type=pl.DeviceIdType.MESH))
    for copy in copies[1:] + copies[:1]:
        copy.start()
    for copy in copies:
        copy.wait()


def kernel(nbatch, members, width, scal_ref, obs_ref, state_ref, out_ref,
           z_ref, pos_ref, info_ref, lhs_ref, inc_ref, pk_ref, wk_ref):
    cells = state_ref.shape[1]
    first = nbatch * width
    total = first + cells
    depth = lhs_ref.shape[1]
    pad = depth - 3 * members

    for b in range(nbatch):
        cols = pl.ds(b * width, width)
        block = obs_ref[b]
        z_ref[:, cols] = block[:members]
        info_ref[b] = block[members:]
        pos_ref[:, cols] = jnp.broadcast_to(block[members + 2 : members + 3], (8, width))
    z_ref[:, first:] = state_ref[...]
    cell = scal_ref[0] + lax.broadcasted_iota(jnp.int32, (8, cells), 1)
    pos_ref[:, first:] = cell.astype(F32)

    def step(b, carry):
        cols = pl.ds(pl.multiple_of(b * width, width), width)
        now = z_ref[:, cols]
        info = info_ref[b]
        value, noise = info[0:1], info[1:2]
        mean = jnp.sum(now, axis=0, keepdims=True) / members
        anomaly = now - mean
        prior = jnp.sum(anomaly * anomaly, axis=0, keepdims=True) / (members - 1) + EPSILON
        post = 1.0 / (1.0 / prior + 1.0 / noise)
        shift = post * (mean / prior + value / noise) - mean
        factor = jnp.sqrt(post / prior) - 1.0
        increment = shift + factor * anomaly
        inc_high, inc_low = split(increment)
        inc_ref[...] = jnp.concatenate([inc_high, inc_low], axis=0)
        scaled = anomaly * (1.0 / ((members - 1) * prior))
        high = scaled.astype(BF16).astype(F32)
        stacked = jnp.concatenate(
            [high, high, scaled - high, jnp.zeros((pad, width), F32)], axis=0
        )
        lhs_ref[...] = jnp.transpose(stacked).astype(BF16)
        turned = jnp.transpose(jnp.concatenate([info] * (128 // info.shape[0]), axis=0))
        pk_ref[...] = jnp.broadcast_to(turned[:, 2:3], (width, LANES))
        wk_ref[...] = jnp.broadcast_to(turned[:, 3:4], (width, LANES))

        def group(g, inner):
            base = g * (GROUP * LANES)
            spans = [
                pl.ds(pl.multiple_of(base + i * LANES, LANES), LANES) for i in range(GROUP)
            ]
            values = [z_ref[:, span] for span in spans]
            places = [pos_ref[0:1, span] for span in spans]
            lhs = lhs_ref[...]
            inc = inc_ref[...]
            results = []
            for z, place in zip(values, places):
                centered = z - jnp.sum(z, axis=0, keepdims=True) / members
                z_high, z_low = split(centered)
                rhs = jnp.concatenate(
                    [z_high, z_low, z_high, jnp.zeros((pad, LANES), BF16)], axis=0
                )
                cov = jnp.dot(lhs, rhs, preferred_element_type=F32)
                near = jnp.maximum(1.0 - jnp.abs(place - pk_ref[...]) * wk_ref[...], 0.0)
                gain_high, gain_low = split(near * near * cov)
                both = jnp.dot(inc, gain_high, preferred_element_type=F32)
                low = jnp.dot(inc[:members], gain_low, preferred_element_type=F32)
                results.append(z + (both[:members] + (both[members:] + low)))
            for span, result in zip(spans, results):
                z_ref[:, span] = result
            return inner

        lax.fori_loop(((b + 1) * width) // (GROUP * LANES), total // (GROUP * LANES), group, 0)
        return carry

    lax.fori_loop(0, nbatch, step, 0)
    out_ref[...] = z_ref[:, first:]


def on_device(state, obs_rows, obs_value, obs_noise, obs_cell, obs_class, obs_count):
    members = state.shape[0]
    cells = state.shape[2]
    slots = obs_rows.shape[3]
    nbatch = lax.axis_size("region")
    tiles = lax.axis_size("tile")
    region_index = lax.axis_index("region")
    tile_index = lax.axis_index("tile")
    tile_width = cells * nbatch
    width = tiles * slots // 2
    depth = -(-3 * members // 128) * 128
    rows = -(-(members + 5) // 16) * 16
    vmem = pl.BlockSpec(memory_space=pltpu.VMEM)
    smem = pl.BlockSpec(memory_space=pltpu.SMEM)
    gathered = pl.pallas_call(
        functools.partial(gather_kernel, nbatch, tiles, members, width, tile_width),
        out_shape=jax.ShapeDtypeStruct((nbatch, rows, width), F32),
        in_specs=[smem] + [vmem] * 5,
        out_specs=pl.BlockSpec(memory_space=pl.ANY),
        scratch_shapes=[
            pltpu.VMEM((rows, slots), F32),
            pltpu.VMEM((tiles, rows, slots), F32),
            pltpu.VMEM((rows, width), F32),
            pltpu.SemaphoreType.DMA((tiles,)),
            pltpu.SemaphoreType.DMA((tiles,)),
            pltpu.SemaphoreType.DMA((nbatch,)),
            pltpu.SemaphoreType.DMA((nbatch,)),
            pltpu.SemaphoreType.DMA,
        ],
        compiler_params=pltpu.CompilerParams(
            collective_id=0, has_side_effects=True, vmem_limit_bytes=24 * 1024 * 1024),
    )(obs_count, obs_rows[0, :, 0, :], obs_value[0], obs_noise[0], obs_cell[0], obs_class[0])
    scalars = (tile_index * tile_width + region_index * cells).astype(jnp.int32)[None]
    total = nbatch * width + cells
    out = pl.pallas_call(
        functools.partial(kernel, nbatch, members, width),
        out_shape=jax.ShapeDtypeStruct((members, cells), F32),
        in_specs=[smem, vmem, vmem],
        out_specs=vmem,
        scratch_shapes=[
            pltpu.VMEM((members, total), F32),
            pltpu.VMEM((8, total), F32),
            pltpu.VMEM((nbatch, rows - members, width), F32),
            pltpu.VMEM((width, depth), BF16),
            pltpu.VMEM((2 * members, width), BF16),
            pltpu.VMEM((width, LANES), F32),
            pltpu.VMEM((width, LANES), F32),
        ],
        compiler_params=pltpu.CompilerParams(vmem_limit_bytes=40 * 1024 * 1024),
    )(scalars, gathered, state[:, 0, :])
    return out[:, None, :]


def solution(mesh):
    placed = (
        P(None, "tile", "region"),
        P("region", None, "tile", None),
        P("region", "tile", None),
        P("region", "tile", None),
        P("region", "tile", None),
        P("region", "tile", None),
        P("region", "tile"),
    )
    return jax.shard_map(
        on_device, mesh=mesh, in_specs=placed, out_specs=P(None, "tile", "region"), check_vma=False
    )
```

```python
import functools

import jax
import jax.numpy as jnp
from jax import lax
from jax.experimental import pallas as pl
from jax.experimental.pallas import tpu as pltpu
from jax.sharding import PartitionSpec as P

EPSILON = 1e-06
LANES = 256
GROUP = 2
CELL_GROUP = 4
F32 = jnp.float32
BF16 = jnp.bfloat16


def split(x):
    high = x.astype(BF16)
    return high, (x - high.astype(F32)).astype(BF16)


def gather_kernel(nbatch, tiles, members, width, tile_width, count_ref, rows_ref, value_ref,
                  noise_ref, cell_ref, class_ref, out_ref, own_ref, slab_ref, live_ref,
                  tile_send, tile_recv, region_send, region_recv, pass_send, pass_recv,
                  local_sem):
    region = lax.axis_index("region")
    tile = lax.axis_index("tile")
    slots = rows_ref.shape[1]
    barrier = pltpu.get_barrier_semaphore()
    for i in range(1, tiles):
        pl.semaphore_signal(barrier, inc=1, device_id=(region, lax.rem(tile + i, tiles)),
                            device_id_type=pl.DeviceIdType.MESH)
    pairs = nbatch // 2
    sibling = region + 1 - 2 * lax.rem(region, 2)
    for i in range(pairs):
        peer = lax.rem(region + 2 * i, nbatch) if i else sibling
        pl.semaphore_signal(barrier, inc=1, device_id=(peer, tile),
                            device_id_type=pl.DeviceIdType.MESH)

    spot = (tile * tile_width + cell_ref[...]).astype(F32)
    inv = 4.0 / (tile_width * (class_ref[...] + 2).astype(F32))
    count = jnp.full((1, slots), count_ref[0, 0], jnp.int32).astype(F32)
    own_ref[0:members] = rows_ref[...]
    own_ref[members:] = jnp.concatenate(
        [value_ref[...], noise_ref[...], spot, inv, count, jnp.zeros((own_ref.shape[0] - members - 5, slots), F32)], axis=0
    )
    pl.semaphore_wait(barrier, tiles + pairs - 1)

    copies = []
    for i in range(1, tiles):
        copy = pltpu.make_async_remote_copy(
            src_ref=own_ref, dst_ref=slab_ref.at[tile],
            send_sem=tile_send.at[i], recv_sem=tile_recv.at[i],
            device_id=(region, lax.rem(tile + i, tiles)),
            device_id_type=pl.DeviceIdType.MESH)
        copy.start()
        copies.append(copy)
    slab_ref[tile] = own_ref[...]
    for copy in copies:
        copy.wait()

    lane = lax.broadcasted_iota(jnp.int32, (1, slots), 1).astype(F32)
    row = lax.broadcasted_iota(jnp.int32, (width, slots), 0).astype(F32)
    start = jnp.zeros((1, slots), F32)
    picks, parts = [], []
    fill = -3 * own_ref.shape[0] % 16
    for t in range(tiles):
        block = slab_ref[t]
        count = block[members + 4 : members + 5]
        place = jnp.where(lane < count, start + lane, -1.0)
        picks.append(jnp.where(row == place, 1.0, 0.0).astype(BF16))
        start = start + count
        high = block.astype(BF16).astype(F32)
        middle = (block - high).astype(BF16).astype(F32)
        low = block - high - middle
        parts.append(jnp.concatenate([high, middle, low, jnp.zeros((fill, slots), F32)], axis=0))
    moved = lax.dot_general(
        jnp.concatenate(parts, axis=1).astype(BF16), jnp.concatenate(picks, axis=1),
        (((1,), (1,)), ((), ())), preferred_element_type=F32)
    count_rows = own_ref.shape[0]
    live_ref[...] = moved[:count_rows] + (
        moved[count_rows : 2 * count_rows] + moved[2 * count_rows : 3 * count_rows])

    def send(src, block, peer, send_sem, recv_sem):
        copy = pltpu.make_async_remote_copy(
            src_ref=src, dst_ref=out_ref.at[block], send_sem=send_sem, recv_sem=recv_sem,
            device_id=(peer, tile), device_id_type=pl.DeviceIdType.MESH)
        copy.start()
        return copy

    across = [
        send(live_ref, region, lax.rem(region + 2 * i, nbatch), region_send.at[i], region_recv.at[i])
        for i in range(1, pairs)
    ]
    passed = [send(live_ref, region, sibling, pass_send.at[0], pass_recv.at[0])]
    local = pltpu.make_async_copy(live_ref, out_ref.at[region], local_sem)
    local.start()
    for i in range(1, pairs):
        across[i - 1].wait_recv()
        block = lax.rem(region + nbatch - 2 * i, nbatch)
        passed.append(send(out_ref.at[block], block, sibling, pass_send.at[i], pass_recv.at[i]))
    local.wait()
    for copy in across:
        copy.wait_send()
    for copy in passed:
        copy.wait()


def kernel(nbatch, members, width, scal_ref, obs_ref, state_ref, out_ref,
           z_ref, pos_ref, info_ref, lhs_ref, inc_ref, pk_ref, wk_ref):
    cells = state_ref.shape[1]
    first = nbatch * width
    total = first + cells
    depth = lhs_ref.shape[1]
    pad = depth - 3 * members

    for b in range(nbatch):
        cols = pl.ds(b * width, width)
        block = obs_ref[b]
        z_ref[:, cols] = block[:members]
        info_ref[b] = block[members:]
        pos_ref[:, cols] = jnp.broadcast_to(block[members + 2 : members + 3], (8, width))
    z_ref[:, first:] = state_ref[...]
    cell = scal_ref[0] + lax.broadcasted_iota(jnp.int32, (8, cells), 1)
    pos_ref[:, first:] = cell.astype(F32)

    def step(b, carry):
        cols = pl.ds(pl.multiple_of(b * width, width), width)
        now = z_ref[:, cols]
        info = info_ref[b]
        value, noise = info[0:1], info[1:2]
        mean = jnp.sum(now, axis=0, keepdims=True) / members
        anomaly = now - mean
        prior = jnp.sum(anomaly * anomaly, axis=0, keepdims=True) / (members - 1) + EPSILON
        post = 1.0 / (1.0 / prior + 1.0 / noise)
        shift = post * (mean / prior + value / noise) - mean
        factor = jnp.sqrt(post / prior) - 1.0
        increment = shift + factor * anomaly
        inc_high, inc_low = split(increment)
        inc_ref[...] = jnp.concatenate([inc_high, inc_low], axis=0)
        scaled = anomaly * (1.0 / ((members - 1) * prior))
        high = scaled.astype(BF16).astype(F32)
        stacked = jnp.concatenate(
            [high, high, scaled - high, jnp.zeros((pad, width), F32)], axis=0
        )
        lhs_ref[...] = jnp.transpose(stacked).astype(BF16)
        turned = jnp.transpose(jnp.concatenate([info] * (128 // info.shape[0]), axis=0))
        pk_ref[...] = jnp.broadcast_to(turned[:, 2:3], (width, LANES))
        wk_ref[...] = jnp.broadcast_to(turned[:, 3:4], (width, LANES))

        def group(size, offset, g, inner):
            base = offset + g * (size * LANES)
            spans = [
                pl.ds(pl.multiple_of(base + i * LANES, LANES), LANES) for i in range(size)
            ]
            values = [z_ref[:, span] for span in spans]
            places = [pos_ref[0:1, span] for span in spans]
            lhs = lhs_ref[...]
            inc = inc_ref[...]
            results = []
            for z, place in zip(values, places):
                centered = z - jnp.sum(z, axis=0, keepdims=True) / members
                z_high, z_low = split(centered)
                rhs = jnp.concatenate(
                    [z_high, z_low, z_high, jnp.zeros((pad, LANES), BF16)], axis=0
                )
                cov = jnp.dot(lhs, rhs, preferred_element_type=F32)
                near = jnp.maximum(1.0 - jnp.abs(place - pk_ref[...]) * wk_ref[...], 0.0)
                gain_high, gain_low = split(near * near * cov)
                both = jnp.dot(inc, gain_high, preferred_element_type=F32)
                low = jnp.dot(inc[:members], gain_low, preferred_element_type=F32)
                results.append(z + (both[:members] + (both[members:] + low)))
            for span, result in zip(spans, results):
                z_ref[:, span] = result
            return inner

        near_count = GROUP * LANES
        lax.fori_loop(((b + 1) * width) // near_count, first // near_count,
                      functools.partial(group, GROUP, 0), 0)
        lax.fori_loop(0, cells // (CELL_GROUP * LANES),
                      functools.partial(group, CELL_GROUP, first), 0)
        return carry

    lax.fori_loop(0, nbatch, step, 0)
    out_ref[...] = z_ref[:, first:]


def on_device(state, obs_rows, obs_value, obs_noise, obs_cell, obs_class, obs_count):
    members = state.shape[0]
    cells = state.shape[2]
    slots = obs_rows.shape[3]
    nbatch = lax.axis_size("region")
    tiles = lax.axis_size("tile")
    region_index = lax.axis_index("region")
    tile_index = lax.axis_index("tile")
    tile_width = cells * nbatch
    width = tiles * slots // 2
    depth = -(-3 * members // 128) * 128
    rows = -(-(members + 5) // 8) * 8
    vmem = pl.BlockSpec(memory_space=pltpu.VMEM)
    smem = pl.BlockSpec(memory_space=pltpu.SMEM)
    gathered = pl.pallas_call(
        functools.partial(gather_kernel, nbatch, tiles, members, width, tile_width),
        out_shape=jax.ShapeDtypeStruct((nbatch, rows, width), F32),
        in_specs=[smem] + [vmem] * 5,
        out_specs=pl.BlockSpec(memory_space=pl.ANY),
        scratch_shapes=[
            pltpu.VMEM((rows, slots), F32),
            pltpu.VMEM((tiles, rows, slots), F32),
            pltpu.VMEM((rows, width), F32),
            pltpu.SemaphoreType.DMA((tiles,)),
            pltpu.SemaphoreType.DMA((tiles,)),
            pltpu.SemaphoreType.DMA((nbatch // 2,)),
            pltpu.SemaphoreType.DMA((nbatch // 2,)),
            pltpu.SemaphoreType.DMA((nbatch // 2,)),
            pltpu.SemaphoreType.DMA((nbatch // 2,)),
            pltpu.SemaphoreType.DMA,
        ],
        compiler_params=pltpu.CompilerParams(
            collective_id=0, has_side_effects=True, vmem_limit_bytes=24 * 1024 * 1024),
    )(obs_count, obs_rows[0, :, 0, :], obs_value[0], obs_noise[0], obs_cell[0], obs_class[0])
    scalars = (tile_index * tile_width + region_index * cells).astype(jnp.int32)[None]
    total = nbatch * width + cells
    out = pl.pallas_call(
        functools.partial(kernel, nbatch, members, width),
        out_shape=jax.ShapeDtypeStruct((members, cells), F32),
        in_specs=[smem, vmem, vmem],
        out_specs=vmem,
        scratch_shapes=[
            pltpu.VMEM((members, total), F32),
            pltpu.VMEM((8, total), F32),
            pltpu.VMEM((nbatch, rows - members, width), F32),
            pltpu.VMEM((width, depth), BF16),
            pltpu.VMEM((2 * members, width), BF16),
            pltpu.VMEM((width, LANES), F32),
            pltpu.VMEM((width, LANES), F32),
        ],
        compiler_params=pltpu.CompilerParams(vmem_limit_bytes=40 * 1024 * 1024),
    )(scalars, gathered, state[:, 0, :])
    return out[:, None, :]


def solution(mesh):
    placed = (
        P(None, "tile", "region"),
        P("region", None, "tile", None),
        P("region", "tile", None),
        P("region", "tile", None),
        P("region", "tile", None),
        P("region", "tile", None),
        P("region", "tile"),
    )
    return jax.shard_map(
        on_device, mesh=mesh, in_specs=placed, out_specs=P(None, "tile", "region"), check_vma=False
    )
```

```python
import functools

import jax
import jax.numpy as jnp
from jax import lax
from jax.experimental import pallas as pl
from jax.experimental.pallas import tpu as pltpu
from jax.sharding import PartitionSpec as P

EPSILON = 1e-06
LANES = 256
GROUP = 4
CELL_GROUP = 8
F32 = jnp.float32
BF16 = jnp.bfloat16


def split(x):
    high = x.astype(BF16)
    return high, (x - high.astype(F32)).astype(BF16)


def gather_kernel(nbatch, tiles, members, width, tile_width, count_ref, rows_ref, value_ref,
                  noise_ref, cell_ref, class_ref, out_ref, own_ref, slab_ref, live_ref,
                  tile_send, tile_recv, region_send, region_recv, pass_send, pass_recv,
                  local_sem):
    region = lax.axis_index("region")
    tile = lax.axis_index("tile")
    slots = rows_ref.shape[1]
    barrier = pltpu.get_barrier_semaphore()
    for i in range(1, tiles):
        pl.semaphore_signal(barrier, inc=1, device_id=(region, lax.rem(tile + i, tiles)),
                            device_id_type=pl.DeviceIdType.MESH)
    pairs = nbatch // 2
    sibling = region + 1 - 2 * lax.rem(region, 2)
    for i in range(pairs):
        peer = lax.rem(region + 2 * i, nbatch) if i else sibling
        pl.semaphore_signal(barrier, inc=1, device_id=(peer, tile),
                            device_id_type=pl.DeviceIdType.MESH)

    spot = (tile * tile_width + cell_ref[...]).astype(F32)
    inv = 4.0 / (tile_width * (class_ref[...] + 2).astype(F32))
    count = jnp.full((1, slots), count_ref[0, 0], jnp.int32).astype(F32)
    own_ref[0:members] = rows_ref[...]
    own_ref[members:] = jnp.concatenate(
        [value_ref[...], noise_ref[...], spot, inv, count, jnp.zeros((own_ref.shape[0] - members - 5, slots), F32)], axis=0
    )
    pl.semaphore_wait(barrier, tiles + pairs - 1)

    copies = []
    for i in range(1, tiles):
        copy = pltpu.make_async_remote_copy(
            src_ref=own_ref, dst_ref=slab_ref.at[tile],
            send_sem=tile_send.at[i], recv_sem=tile_recv.at[i],
            device_id=(region, lax.rem(tile + i, tiles)),
            device_id_type=pl.DeviceIdType.MESH)
        copy.start()
        copies.append(copy)
    slab_ref[tile] = own_ref[...]
    for copy in copies:
        copy.wait()

    lane = lax.broadcasted_iota(jnp.int32, (1, slots), 1).astype(F32)
    row = lax.broadcasted_iota(jnp.int32, (width, slots), 0).astype(F32)
    start = jnp.zeros((1, slots), F32)
    picks, parts = [], []
    fill = -3 * own_ref.shape[0] % 16
    for t in range(tiles):
        block = slab_ref[t]
        count = block[members + 4 : members + 5]
        place = jnp.where(lane < count, start + lane, -1.0)
        picks.append(jnp.where(row == place, 1.0, 0.0).astype(BF16))
        start = start + count
        high = block.astype(BF16).astype(F32)
        middle = (block - high).astype(BF16).astype(F32)
        low = block - high - middle
        parts.append(jnp.concatenate([high, middle, low, jnp.zeros((fill, slots), F32)], axis=0))
    moved = lax.dot_general(
        jnp.concatenate(parts, axis=1).astype(BF16), jnp.concatenate(picks, axis=1),
        (((1,), (1,)), ((), ())), preferred_element_type=F32)
    count_rows = own_ref.shape[0]
    live_ref[...] = moved[:count_rows] + (
        moved[count_rows : 2 * count_rows] + moved[2 * count_rows : 3 * count_rows])

    def send(src, block, peer, send_sem, recv_sem):
        copy = pltpu.make_async_remote_copy(
            src_ref=src, dst_ref=out_ref.at[block], send_sem=send_sem, recv_sem=recv_sem,
            device_id=(peer, tile), device_id_type=pl.DeviceIdType.MESH)
        copy.start()
        return copy

    across = [
        send(live_ref, region, lax.rem(region + 2 * i, nbatch), region_send.at[i], region_recv.at[i])
        for i in range(1, pairs)
    ]
    passed = [send(live_ref, region, sibling, pass_send.at[0], pass_recv.at[0])]
    local = pltpu.make_async_copy(live_ref, out_ref.at[region], local_sem)
    local.start()
    for i in range(1, pairs):
        across[i - 1].wait_recv()
        block = lax.rem(region + nbatch - 2 * i, nbatch)
        passed.append(send(out_ref.at[block], block, sibling, pass_send.at[i], pass_recv.at[i]))
    local.wait()
    for copy in across:
        copy.wait_send()
    for copy in passed:
        copy.wait()


def kernel(nbatch, members, width, scal_ref, obs_ref, state_ref, out_ref,
           z_ref, pos_ref, info_ref, lhs_ref, inc_ref, pk_ref, wk_ref):
    cells = state_ref.shape[1]
    first = nbatch * width
    total = first + cells
    depth = lhs_ref.shape[1]
    pad = depth - 3 * members

    for b in range(nbatch):
        cols = pl.ds(b * width, width)
        block = obs_ref[b]
        z_ref[:, cols] = block[:members]
        info_ref[b] = block[members:]
        pos_ref[:, cols] = jnp.broadcast_to(block[members + 2 : members + 3], (8, width))
    z_ref[:, first:] = state_ref[...]
    cell = scal_ref[0] + lax.broadcasted_iota(jnp.int32, (8, cells), 1)
    pos_ref[:, first:] = cell.astype(F32)

    def prepare(b):
        cols = pl.ds(pl.multiple_of(b * width, width), width)
        now = z_ref[:, cols]
        info = info_ref[b]
        value, noise = info[0:1], info[1:2]
        mean = jnp.sum(now, axis=0, keepdims=True) / members
        anomaly = now - mean
        prior = jnp.sum(anomaly * anomaly, axis=0, keepdims=True) / (members - 1) + EPSILON
        post = 1.0 / (1.0 / prior + 1.0 / noise)
        shift = post * (mean / prior + value / noise) - mean
        factor = jnp.sqrt(post / prior) - 1.0
        increment = shift + factor * anomaly
        inc_high, inc_low = split(increment)
        inc = jnp.concatenate([inc_high, inc_low], axis=0)
        scaled = anomaly * (1.0 / ((members - 1) * prior))
        high = scaled.astype(BF16).astype(F32)
        stacked = jnp.concatenate(
            [high, high, scaled - high, jnp.zeros((pad, width), F32)], axis=0
        )
        lhs = jnp.transpose(stacked).astype(BF16)
        turned = jnp.transpose(jnp.concatenate([info] * (128 // info.shape[0]), axis=0))
        pk = jnp.broadcast_to(turned[:, 2:3], (width, LANES))
        wk = jnp.broadcast_to(turned[:, 3:4], (width, LANES))
        return lhs, inc, pk, wk

    def keep(terms):
        lhs_ref[...], inc_ref[...], pk_ref[...], wk_ref[...] = terms

    def step(b, carry):
        def group(size, offset, following, g, inner):
            base = offset + g * (size * LANES)
            spans = [
                pl.ds(pl.multiple_of(base + i * LANES, LANES), LANES) for i in range(size)
            ]
            if following is not None:
                terms = prepare(following)
            values = [z_ref[:, span] for span in spans]
            places = [pos_ref[0:1, span] for span in spans]
            lhs = lhs_ref[...]
            inc = inc_ref[...]
            results = []
            for z, place in zip(values, places):
                centered = z - jnp.sum(z, axis=0, keepdims=True) / members
                z_high, z_low = split(centered)
                rhs = jnp.concatenate(
                    [z_high, z_low, z_high, jnp.zeros((pad, LANES), BF16)], axis=0
                )
                cov = jnp.dot(lhs, rhs, preferred_element_type=F32)
                near = jnp.maximum(1.0 - jnp.abs(place - pk_ref[...]) * wk_ref[...], 0.0)
                gain_high, gain_low = split(near * near * cov)
                both = jnp.dot(inc, gain_high, preferred_element_type=F32)
                low = jnp.dot(inc[:members], gain_low, preferred_element_type=F32)
                results.append(z + (both[:members] + (both[members:] + low)))
            for span, result in zip(spans, results):
                z_ref[:, span] = result
            if following is not None:
                keep(terms)
            return inner

        near_count = GROUP * LANES
        lax.fori_loop(((b + 1) * width) // near_count, first // near_count,
                      functools.partial(group, GROUP, 0, None), 0)
        bodies = cells // (CELL_GROUP * LANES)
        if bodies > 1:
            lax.fori_loop(0, bodies - 1,
                          functools.partial(group, CELL_GROUP, first, None), 0)
        group(CELL_GROUP, first, jnp.minimum(b + 1, nbatch - 1), bodies - 1, 0)
        return carry

    keep(prepare(0))
    lax.fori_loop(0, nbatch, step, 0)
    out_ref[...] = z_ref[:, first:]


def on_device(state, obs_rows, obs_value, obs_noise, obs_cell, obs_class, obs_count):
    members = state.shape[0]
    cells = state.shape[2]
    slots = obs_rows.shape[3]
    nbatch = lax.axis_size("region")
    tiles = lax.axis_size("tile")
    region_index = lax.axis_index("region")
    tile_index = lax.axis_index("tile")
    tile_width = cells * nbatch
    width = tiles * slots // 2
    depth = -(-3 * members // 128) * 128
    rows = -(-(members + 5) // 8) * 8
    vmem = pl.BlockSpec(memory_space=pltpu.VMEM)
    smem = pl.BlockSpec(memory_space=pltpu.SMEM)
    gathered = pl.pallas_call(
        functools.partial(gather_kernel, nbatch, tiles, members, width, tile_width),
        out_shape=jax.ShapeDtypeStruct((nbatch, rows, width), F32),
        in_specs=[smem] + [vmem] * 5,
        out_specs=pl.BlockSpec(memory_space=pl.ANY),
        scratch_shapes=[
            pltpu.VMEM((rows, slots), F32),
            pltpu.VMEM((tiles, rows, slots), F32),
            pltpu.VMEM((rows, width), F32),
            pltpu.SemaphoreType.DMA((tiles,)),
            pltpu.SemaphoreType.DMA((tiles,)),
            pltpu.SemaphoreType.DMA((nbatch // 2,)),
            pltpu.SemaphoreType.DMA((nbatch // 2,)),
            pltpu.SemaphoreType.DMA((nbatch // 2,)),
            pltpu.SemaphoreType.DMA((nbatch // 2,)),
            pltpu.SemaphoreType.DMA,
        ],
        compiler_params=pltpu.CompilerParams(
            collective_id=0, has_side_effects=True, vmem_limit_bytes=24 * 1024 * 1024),
    )(obs_count, obs_rows[0, :, 0, :], obs_value[0], obs_noise[0], obs_cell[0], obs_class[0])
    scalars = (tile_index * tile_width + region_index * cells).astype(jnp.int32)[None]
    total = nbatch * width + cells
    out = pl.pallas_call(
        functools.partial(kernel, nbatch, members, width),
        out_shape=jax.ShapeDtypeStruct((members, cells), F32),
        in_specs=[smem, vmem, vmem],
        out_specs=vmem,
        scratch_shapes=[
            pltpu.VMEM((members, total), F32),
            pltpu.VMEM((8, total), F32),
            pltpu.VMEM((nbatch, rows - members, width), F32),
            pltpu.VMEM((width, depth), BF16),
            pltpu.VMEM((2 * members, width), BF16),
            pltpu.VMEM((width, LANES), F32),
            pltpu.VMEM((width, LANES), F32),
        ],
        compiler_params=pltpu.CompilerParams(vmem_limit_bytes=40 * 1024 * 1024),
    )(scalars, gathered, state[:, 0, :])
    return out[:, None, :]


def solution(mesh):
    placed = (
        P(None, "tile", "region"),
        P("region", None, "tile", None),
        P("region", "tile", None),
        P("region", "tile", None),
        P("region", "tile", None),
        P("region", "tile", None),
        P("region", "tile"),
    )
    return jax.shard_map(
        on_device, mesh=mesh, in_specs=placed, out_specs=P(None, "tile", "region"), check_vma=False
    )
```

```python
import functools

import jax
import jax.numpy as jnp
from jax import lax
from jax.experimental import pallas as pl
from jax.experimental.pallas import tpu as pltpu
from jax.sharding import PartitionSpec as P

EPSILON = 1e-06
LANES = 256
GROUP = 2
CELL_GROUP = 8
F32 = jnp.float32
BF16 = jnp.bfloat16


def split(x):
    high = x.astype(BF16)
    return high, (x - high.astype(F32)).astype(BF16)


def gather_kernel(nbatch, tiles, members, width, tile_width, count_ref, rows_ref, value_ref,
                  noise_ref, cell_ref, class_ref, out_ref, own_ref, slab_ref, live_ref,
                  tile_send, tile_recv, region_send, region_recv, pass_send, pass_recv,
                  local_sem):
    region = lax.axis_index("region")
    tile = lax.axis_index("tile")
    slots = rows_ref.shape[1]
    barrier = pltpu.get_barrier_semaphore()
    for i in range(1, tiles):
        pl.semaphore_signal(barrier, inc=1, device_id=(region, lax.rem(tile + i, tiles)),
                            device_id_type=pl.DeviceIdType.MESH)
    pairs = nbatch // 2
    sibling = region + 1 - 2 * lax.rem(region, 2)
    for i in range(pairs):
        peer = lax.rem(region + 2 * i, nbatch) if i else sibling
        pl.semaphore_signal(barrier, inc=1, device_id=(peer, tile),
                            device_id_type=pl.DeviceIdType.MESH)

    spot = (tile * tile_width + cell_ref[...]).astype(F32)
    inv = 4.0 / (tile_width * (class_ref[...] + 2).astype(F32))
    count = jnp.full((1, slots), count_ref[0, 0], jnp.int32).astype(F32)
    own_ref[0:members] = rows_ref[...]
    own_ref[members:] = jnp.concatenate(
        [value_ref[...], noise_ref[...], spot, inv, count, jnp.zeros((own_ref.shape[0] - members - 5, slots), F32)], axis=0
    )
    pl.semaphore_wait(barrier, tiles + pairs - 1)

    copies = []
    for i in range(1, tiles):
        copy = pltpu.make_async_remote_copy(
            src_ref=own_ref, dst_ref=slab_ref.at[tile],
            send_sem=tile_send.at[i], recv_sem=tile_recv.at[i],
            device_id=(region, lax.rem(tile + i, tiles)),
            device_id_type=pl.DeviceIdType.MESH)
        copy.start()
        copies.append(copy)
    slab_ref[tile] = own_ref[...]
    for copy in copies:
        copy.wait()

    lane = lax.broadcasted_iota(jnp.int32, (1, slots), 1).astype(F32)
    row = lax.broadcasted_iota(jnp.int32, (width, slots), 0).astype(F32)
    start = jnp.zeros((1, slots), F32)
    picks, parts = [], []
    fill = -3 * own_ref.shape[0] % 16
    for t in range(tiles):
        block = slab_ref[t]
        count = block[members + 4 : members + 5]
        place = jnp.where(lane < count, start + lane, -1.0)
        picks.append(jnp.where(row == place, 1.0, 0.0).astype(BF16))
        start = start + count
        high = block.astype(BF16).astype(F32)
        middle = (block - high).astype(BF16).astype(F32)
        low = block - high - middle
        parts.append(jnp.concatenate([high, middle, low, jnp.zeros((fill, slots), F32)], axis=0))
    moved = lax.dot_general(
        jnp.concatenate(parts, axis=1).astype(BF16), jnp.concatenate(picks, axis=1),
        (((1,), (1,)), ((), ())), preferred_element_type=F32)
    count_rows = own_ref.shape[0]
    live_ref[...] = moved[:count_rows] + (
        moved[count_rows : 2 * count_rows] + moved[2 * count_rows : 3 * count_rows])

    def send(src, block, peer, send_sem, recv_sem):
        copy = pltpu.make_async_remote_copy(
            src_ref=src, dst_ref=out_ref.at[block], send_sem=send_sem, recv_sem=recv_sem,
            device_id=(peer, tile), device_id_type=pl.DeviceIdType.MESH)
        copy.start()
        return copy

    across = [
        send(live_ref, region, lax.rem(region + 2 * i, nbatch), region_send.at[i], region_recv.at[i])
        for i in range(1, pairs)
    ]
    passed = [send(live_ref, region, sibling, pass_send.at[0], pass_recv.at[0])]
    local = pltpu.make_async_copy(live_ref, out_ref.at[region], local_sem)
    local.start()
    for i in range(1, pairs):
        across[i - 1].wait_recv()
        block = lax.rem(region + nbatch - 2 * i, nbatch)
        passed.append(send(out_ref.at[block], block, sibling, pass_send.at[i], pass_recv.at[i]))
    local.wait()
    for copy in across:
        copy.wait_send()
    for copy in passed:
        copy.wait()


def kernel(nbatch, members, width, scal_ref, obs_ref, state_ref, out_ref,
           z_ref, pos_ref, info_ref, lhs_ref, inc_ref, pk_ref, wk_ref):
    cells = state_ref.shape[1]
    first = nbatch * width
    total = first + cells
    depth = lhs_ref.shape[1]
    pad = depth - 3 * members

    for b in range(nbatch):
        cols = pl.ds(b * width, width)
        block = obs_ref[b]
        z_ref[:, cols] = block[:members]
        info_ref[b] = block[members:]
        pos_ref[:, cols] = jnp.broadcast_to(block[members + 2 : members + 3], (8, width))
    z_ref[:, first:] = state_ref[...]
    cell = scal_ref[0] + lax.broadcasted_iota(jnp.int32, (8, cells), 1)
    pos_ref[:, first:] = cell.astype(F32)

    def prepare(b):
        cols = pl.ds(pl.multiple_of(b * width, width), width)
        now = z_ref[:, cols]
        info = info_ref[b]
        value, noise = info[0:1], info[1:2]
        mean = jnp.sum(now, axis=0, keepdims=True) / members
        anomaly = now - mean
        prior = jnp.sum(anomaly * anomaly, axis=0, keepdims=True) / (members - 1) + EPSILON
        post = 1.0 / (1.0 / prior + 1.0 / noise)
        shift = post * (mean / prior + value / noise) - mean
        factor = jnp.sqrt(post / prior) - 1.0
        increment = shift + factor * anomaly
        inc_high, inc_low = split(increment)
        inc = jnp.concatenate([inc_high, inc_low], axis=0)
        scaled = anomaly * (1.0 / ((members - 1) * prior))
        high = scaled.astype(BF16).astype(F32)
        stacked = jnp.concatenate(
            [high, high, scaled - high, jnp.zeros((pad, width), F32)], axis=0
        )
        lhs = jnp.transpose(stacked).astype(BF16)
        turned = jnp.transpose(jnp.concatenate([info] * (128 // info.shape[0]), axis=0))
        pk = jnp.broadcast_to(turned[:, 2:3], (width, LANES))
        wk = jnp.broadcast_to(turned[:, 3:4], (width, LANES))
        return lhs, inc, pk, wk

    def keep(terms):
        lhs_ref[...], inc_ref[...], pk_ref[...], wk_ref[...] = terms

    def step(b, carry):
        def group(size, offset, following, g, inner):
            base = offset + g * (size * LANES)
            spans = [
                pl.ds(pl.multiple_of(base + i * LANES, LANES), LANES) for i in range(size)
            ]
            if following is not None:
                terms = prepare(following)
            values = [z_ref[:, span] for span in spans]
            places = [pos_ref[0:1, span] for span in spans]
            lhs = lhs_ref[...]
            inc = inc_ref[...]
            results = []
            for z, place in zip(values, places):
                centered = z - jnp.sum(z, axis=0, keepdims=True) / members
                z_high, z_low = split(centered)
                rhs = jnp.concatenate(
                    [z_high, z_low, z_high, jnp.zeros((pad, LANES), BF16)], axis=0
                )
                cov = jnp.dot(lhs, rhs, preferred_element_type=F32)
                near = jnp.maximum(1.0 - jnp.abs(place - pk_ref[...]) * wk_ref[...], 0.0)
                gain_high, gain_low = split(near * near * cov)
                both = jnp.dot(inc, gain_high, preferred_element_type=F32)
                low = jnp.dot(inc[:members], gain_low, preferred_element_type=F32)
                results.append(z + (both[:members] + (both[members:] + low)))
            for span, result in zip(spans, results):
                z_ref[:, span] = result
            if following is not None:
                keep(terms)
            return inner

        near_count = GROUP * LANES
        lax.fori_loop(((b + 1) * width) // near_count, first // near_count,
                      functools.partial(group, GROUP, 0, None), 0)
        bodies = cells // (CELL_GROUP * LANES)
        if bodies > 1:
            lax.fori_loop(0, bodies - 1,
                          functools.partial(group, CELL_GROUP, first, None), 0)
        group(CELL_GROUP, first, jnp.minimum(b + 1, nbatch - 1), bodies - 1, 0)
        return carry

    keep(prepare(0))
    lax.fori_loop(0, nbatch, step, 0)
    out_ref[...] = z_ref[:, first:]


def on_device(state, obs_rows, obs_value, obs_noise, obs_cell, obs_class, obs_count):
    members = state.shape[0]
    cells = state.shape[2]
    slots = obs_rows.shape[3]
    nbatch = lax.axis_size("region")
    tiles = lax.axis_size("tile")
    region_index = lax.axis_index("region")
    tile_index = lax.axis_index("tile")
    tile_width = cells * nbatch
    width = tiles * slots // 2
    depth = -(-3 * members // 128) * 128
    rows = -(-(members + 5) // 8) * 8
    vmem = pl.BlockSpec(memory_space=pltpu.VMEM)
    smem = pl.BlockSpec(memory_space=pltpu.SMEM)
    gathered = pl.pallas_call(
        functools.partial(gather_kernel, nbatch, tiles, members, width, tile_width),
        out_shape=jax.ShapeDtypeStruct((nbatch, rows, width), F32),
        in_specs=[smem] + [vmem] * 5,
        out_specs=pl.BlockSpec(memory_space=pl.ANY),
        scratch_shapes=[
            pltpu.VMEM((rows, slots), F32),
            pltpu.VMEM((tiles, rows, slots), F32),
            pltpu.VMEM((rows, width), F32),
            pltpu.SemaphoreType.DMA((tiles,)),
            pltpu.SemaphoreType.DMA((tiles,)),
            pltpu.SemaphoreType.DMA((nbatch // 2,)),
            pltpu.SemaphoreType.DMA((nbatch // 2,)),
            pltpu.SemaphoreType.DMA((nbatch // 2,)),
            pltpu.SemaphoreType.DMA((nbatch // 2,)),
            pltpu.SemaphoreType.DMA,
        ],
        compiler_params=pltpu.CompilerParams(
            collective_id=0, has_side_effects=True, vmem_limit_bytes=24 * 1024 * 1024),
    )(obs_count, obs_rows[0, :, 0, :], obs_value[0], obs_noise[0], obs_cell[0], obs_class[0])
    scalars = (tile_index * tile_width + region_index * cells).astype(jnp.int32)[None]
    total = nbatch * width + cells
    out = pl.pallas_call(
        functools.partial(kernel, nbatch, members, width),
        out_shape=jax.ShapeDtypeStruct((members, cells), F32),
        in_specs=[smem, vmem, vmem],
        out_specs=vmem,
        scratch_shapes=[
            pltpu.VMEM((members, total), F32),
            pltpu.VMEM((8, total), F32),
            pltpu.VMEM((nbatch, rows - members, width), F32),
            pltpu.VMEM((width, depth), BF16),
            pltpu.VMEM((2 * members, width), BF16),
            pltpu.VMEM((width, LANES), F32),
            pltpu.VMEM((width, LANES), F32),
        ],
        compiler_params=pltpu.CompilerParams(vmem_limit_bytes=40 * 1024 * 1024),
    )(scalars, gathered, state[:, 0, :])
    return out[:, None, :]


def solution(mesh):
    placed = (
        P(None, "tile", "region"),
        P("region", None, "tile", None),
        P("region", "tile", None),
        P("region", "tile", None),
        P("region", "tile", None),
        P("region", "tile", None),
        P("region", "tile"),
    )
    return jax.shard_map(
        on_device, mesh=mesh, in_specs=placed, out_specs=P(None, "tile", "region"), check_vma=False
    )
```
